32 devices in a mesh: flow: 4 (over y, core), link: 8 (over z, x).
Axes of the slice: x: 2, y: 2, z: 4, core: 2. Of those that a mesh axis runs over, the one named last changes fastest.
Arguments:
- route_tiles: bfloat16 [512, 1024, 128], P('flow', 'link'), may hold values from 0 to 1, as said below
- tile_count: int32 [4, 8], P('flow', 'link'), may hold values from 16 to 128, as said below
- tile_flow: int32 [4, 1024], P('flow', 'link'), may hold values from 0 to 1023
- tile_link: int32 [4, 1024], P('flow', 'link'), may hold values from 0 to 511, as said below
- flow_class: int32 [524288], P('flow'), may hold values from 0 to 255
- class_weight: float32 [256], replicated, may hold values from 0.25 to 4
- access_price: float32 [524288], P('flow'), may hold values from 0.5 to 4
- capacity: float32 [524288], P('link'), may hold values from 1 to 8
- init_price: float32 [524288], P('link'), may hold values from 0.5 to 2
Outputs:
- flow_rate: float32 [524288], P('flow')
- link_price: float32 [524288], P('link')
The draws below stay inside these ranges and needn't reach their ends.
Inputs may be any that keep to these rules, and one draw needn't show every extreme that they name: `route_tiles`: entries are 0 or 1. `tile_count`: counts follow 128 divided by 1, 2, 4 or 8; some device uses all 128 slots in every draw. `tile_link`: within one device's slots no link block repeats.
All inputs are finite; a program needn't handle non-finite values.
Results may differ from the reference program's by a relative error of at most 0.0014.
Values may be sent and summed in bfloat16 or wider, within the bound.
A program may use at most 64 MiB of HBM per device.

```python
import math
import jax
import jax.numpy as jnp
from jax import lax

TILE = 128
CLASSES = 256
FB_G = 1024
LB_G = 512
CAP = 128
ITERS = 2
FLOWS = 524288
LINKS = 524288
N_FLOW = 4
N_LINK = 8


def draw_route_tiles(key, part):
    picks = jax.random.randint(key, (N_FLOW * CAP, N_LINK * TILE, TILE), 0, 16)
    return (picks == 0).astype(jnp.float32).astype(jnp.bfloat16)


def draw_tile_count(key, part):
    powers = jax.random.randint(key, (N_FLOW * N_LINK,), 0, 4)
    counts = CAP // jnp.power(2, powers).astype(jnp.int32)
    picked = jax.random.randint(jax.random.fold_in(key, 1), (), 0, N_FLOW * N_LINK)
    counts = jnp.where(jnp.arange(N_FLOW * N_LINK) == picked, CAP, counts)
    return counts.reshape(N_FLOW, N_LINK).astype(jnp.int32)


def draw_tile_link(key, part):
    keys = jax.random.split(key, N_FLOW * N_LINK)
    picks = jax.vmap(lambda k: jax.random.permutation(k, LB_G)[:CAP])(keys)
    return picks.reshape(N_FLOW, N_LINK * CAP).astype(jnp.int32)


def with_ends(array, rng, low, largest):
    shape = array.shape
    index_at = [jax.random.randint(jax.random.fold_in(rng, axis), (), 0, shape[axis]) for axis in range(len(shape))]
    array = array.at[tuple(index_at)].set(low)
    longest = shape.index(max(shape))
    index_at[longest] = (index_at[longest] + 1) % shape[longest]
    return array.at[tuple(index_at)].set(largest)


def shard_levels(own_key, dims, cuts, low, high):
    gain, own = 1.0, jax.random.fold_in(own_key, 6)
    for axis_at, parts in cuts:
        steps = jnp.exp(jax.random.uniform(jax.random.fold_in(own, axis_at), (parts,), jnp.float32, low / len(cuts), high / len(cuts)))
        gain = gain * jnp.repeat(steps, dims[axis_at] // parts).reshape([-1 if axis == axis_at else 1 for axis in range(len(dims))])
    return gain


def setup_inputs(seed: int = 0) -> dict:
    streams_of = jax.random.split(jax.random.key(seed), 10)
    return {
        "route_tiles": draw_route_tiles(jax.random.fold_in(streams_of[9], 71), 0),
        "tile_count": draw_tile_count(jax.random.fold_in(streams_of[9], 71), 0),
        "tile_flow": with_ends(jax.random.randint(streams_of[2], (N_FLOW, N_LINK * CAP), 0, FB_G), jax.random.fold_in(streams_of[2], 1), 0, FB_G - 1).astype(jnp.int32),
        "tile_link": draw_tile_link(jax.random.fold_in(streams_of[9], 71), 0),
        "flow_class": with_ends(jax.random.randint(streams_of[4], (FLOWS,), 0, CLASSES), jax.random.fold_in(streams_of[4], 1), 0, CLASSES - 1).astype(jnp.int32),
        "class_weight": jnp.clip(jnp.exp(jax.random.uniform(streams_of[5], (CLASSES,), jnp.float32, math.log(0.25), math.log(4.0))), 0.25, 4.0),
        "access_price": jnp.clip(jnp.exp(math.log(4.0) - 2.0794415 * jax.random.uniform(streams_of[6], (FLOWS,), jnp.float32) ** shard_levels(streams_of[6], (FLOWS,), ((0, 4),), -0.2, 0.2)), 0.5, 4.0),
        "capacity": jnp.clip(jnp.exp(math.log(8.0) - 2.0794415 * jax.random.uniform(streams_of[7], (LINKS,), jnp.float32) ** shard_levels(streams_of[7], (LINKS,), ((0, 8),), -0.2, 0.2)), 1.0, 8.0),
        "init_price": jnp.clip(jnp.exp(math.log(2.0) - 1.3862944 * jax.random.uniform(streams_of[8], (LINKS,), jnp.float32) ** shard_levels(streams_of[8], (LINKS,), ((0, 8),), -0.2, 0.2)), 0.5, 2.0),
    }


step_size = 0.5


def reference(route_tiles, tile_count, tile_flow, tile_link, flow_class, class_weight, access_price, capacity, init_price):
    devices_all = N_FLOW * N_LINK
    tiles = route_tiles.reshape(N_FLOW, CAP, N_LINK, TILE, TILE).transpose(0, 2, 1, 3, 4).reshape(devices_all, CAP, TILE, TILE)
    flow_idx = tile_flow.reshape(N_FLOW, N_LINK, CAP) + (jnp.arange(N_FLOW, dtype=jnp.int32) * FB_G)[:, None, None]
    link_idx = tile_link.reshape(N_FLOW, N_LINK, CAP) + (jnp.arange(N_LINK, dtype=jnp.int32) * LB_G)[None, :, None]
    flow_idx = flow_idx.reshape(devices_all, CAP).astype(jnp.int32)
    link_idx = link_idx.reshape(devices_all, CAP).astype(jnp.int32)
    valid = (jnp.arange(CAP, dtype=jnp.int32)[None, :] < tile_count.reshape(devices_all, 1)).astype(jnp.float32)
    weight = class_weight[flow_class].reshape(N_FLOW * FB_G, TILE)
    access = access_price.reshape(N_FLOW * FB_G, TILE)
    link_cap = capacity.reshape(N_LINK * LB_G, TILE)
    price = init_price.reshape(N_LINK * LB_G, TILE)

    def route_sums(price_b):
        def one(total, item):
            tile_set, fl, li, mask = item
            gathered = price_b[li].astype(jnp.float32)
            term = jnp.einsum("sab,sa->sb", tile_set.astype(jnp.float32), gathered) * mask[:, None]
            return total.at[fl].add(term), None
        start = jnp.zeros((N_FLOW * FB_G, TILE), jnp.float32)
        return lax.scan(one, start, (tiles, flow_idx, link_idx, valid))[0]

    def load_sums(rate_b):
        def one(total, item):
            tile_set, fl, li, mask = item
            gathered = rate_b[fl].astype(jnp.float32)
            term = jnp.einsum("sab,sb->sa", tile_set.astype(jnp.float32), gathered) * mask[:, None]
            return total.at[li].add(term), None
        start = jnp.zeros((N_LINK * LB_G, TILE), jnp.float32)
        return lax.scan(one, start, (tiles, flow_idx, link_idx, valid))[0]

    rate = jnp.zeros_like(weight)
    for step in range(ITERS):
        route_sum = route_sums(price.astype(jnp.bfloat16))
        rate = weight / (access + route_sum)
        load = load_sums(rate.astype(jnp.bfloat16))
        price = price * jnp.exp(step_size * (load / link_cap - 1.0))
    return rate.reshape(-1), price.reshape(-1)
```

```python
import functools

import jax
import jax.numpy as jnp
from jax import lax
from jax.experimental import pallas as pl
from jax.experimental.pallas import tpu as pltpu
from jax.sharding import PartitionSpec as P

ITERS = 2
STEP = 0.5
GROUP = 16
F32, BF16 = jnp.float32, jnp.bfloat16


def iota(shape, dim):
    return lax.broadcasted_iota(jnp.int32, shape, dim)


def halves(x):
    high = x.astype(BF16)
    low = (x - high.astype(F32)).astype(BF16)
    return high, low


def kernel(
    n_flow, n_link,
    tiles_hbm, count_ref, flow_smem, flow_ref, link_ref, class_ref, table_ref, access_ref, cap_ref, price_ref,
    rate_out, price_out,
    tiles, flow_all, link_all, route_buf, load_buf, picked, term, rate_b, match, parts, own_class, own_access, price,
    tile_sem, idx_send, flow_recv, link_recv, route_send, route_recv, load_send, load_recv,
):
    slots, size = tiles.shape[0], tiles.shape[1]
    link_blocks, flow_blocks = price_ref.shape[0], access_ref.shape[0]
    me_f, me_l = lax.axis_index("flow"), lax.axis_index("link")
    barrier = pltpu.get_barrier_semaphore()
    link_peers = [lax.rem(me_l + k, n_link) for k in range(1, n_link)]
    flow_peers = [lax.rem(me_f + k, n_flow) for k in range(1, n_flow)]
    for peer in link_peers:
        pl.semaphore_signal(barrier, inc=1, device_id={"link": peer})
    for peer in flow_peers:
        pl.semaphore_signal(barrier, inc=1, device_id={"flow": peer})

    chunk = slots // tile_sem.shape[0]
    loads = []
    for c in range(tile_sem.shape[0]):
        copy = pltpu.make_async_copy(
            tiles_hbm.at[pl.ds(c * chunk, chunk)], tiles.at[pl.ds(c * chunk, chunk)], tile_sem.at[c]
        )
        copy.start()
        loads.append(copy)

    count = count_ref[0, 0]
    used = iota((8, slots), 1) < count
    flow_all[me_l] = jnp.where(used, jnp.broadcast_to(flow_ref[...], (8, slots)), -1)
    link_all[me_f] = jnp.where(used, jnp.broadcast_to(link_ref[...], (8, slots)), -1)
    pl.semaphore_wait(barrier, n_link + n_flow - 2)

    def to_link(buf, send, recv):
        return [
            pltpu.make_async_remote_copy(
                src_ref=buf.at[me_l], dst_ref=buf.at[me_l], send_sem=send.at[k], recv_sem=recv.at[me_l],
                device_id={"link": peer}, device_id_type=pl.DeviceIdType.MESH,
            )
            for k, peer in enumerate(link_peers)
        ]

    def to_flow(buf, send, recv):
        return [
            pltpu.make_async_remote_copy(
                src_ref=buf.at[me_f], dst_ref=buf.at[me_f], send_sem=send.at[k], recv_sem=recv.at[me_f],
                device_id={"flow": peer}, device_id_type=pl.DeviceIdType.MESH,
            )
            for k, peer in enumerate(flow_peers)
        ]

    def arrived(buf, send, recv, k, source, axis):
        pltpu.make_async_remote_copy(
            src_ref=buf.at[source], dst_ref=buf.at[source], send_sem=send.at[k], recv_sem=recv.at[source],
            device_id={axis: source}, device_id_type=pl.DeviceIdType.MESH,
        ).wait_recv()

    link_sources = [lax.rem(me_l + n_link - k, n_link) for k in range(1, n_link)]
    flow_sources = [lax.rem(me_f + n_flow - k, n_flow) for k in range(1, n_flow)]
    pending = to_link(flow_all, idx_send.at[0], flow_recv) + to_flow(link_all, idx_send.at[1], link_recv)
    for copy in pending:
        copy.start()

    def column(row):
        return jnp.broadcast_to(row.astype(F32), (slots, slots)).T

    lane = iota((slots, slots), 1)
    link_col = column(link_ref[...])
    pick = jnp.concatenate(
        [(link_col == (lane + k * slots).astype(F32)).astype(BF16) for k in range(link_blocks // slots)], axis=1
    )
    row_used = iota((slots, size), 0) < count
    group_row = iota((GROUP, size), 0)

    def route_terms(first):
        def body(g, carry):
            at = pl.multiple_of(g * GROUP, GROUP)
            p = picked[pl.ds(at, GROUP), :]
            left = jnp.concatenate(
                [jnp.where(group_row == k, p, jnp.zeros_like(p)).astype(BF16) for k in range(GROUP)], axis=1
            )
            right = tiles[pl.ds(at, GROUP)].reshape(GROUP * size, size)
            term[pl.ds(at, GROUP), :] = jnp.dot(left, right, preferred_element_type=F32)
            return carry

        if first:
            per = chunk // GROUP
            for c, copy in enumerate(loads):
                copy.wait()
                lax.fori_loop(c * per, (c + 1) * per, body, 0)
        else:
            lax.fori_loop(0, slots // GROUP, body, 0)

    def load_terms():
        def body(g, carry):
            at = pl.multiple_of(g * GROUP, GROUP)
            q = rate_b[pl.ds(at, GROUP), :]
            right = tiles[pl.ds(at, GROUP)].reshape(GROUP * size, size)
            full = lax.dot_general(q, right, (((1,), (1,)), ((), ())), preferred_element_type=F32)
            total = jnp.zeros((GROUP, size), F32)
            for k in range(GROUP):
                total = jnp.where(group_row == k, full[:, k * size : (k + 1) * size], total)
            term[pl.ds(at, GROUP), :] = total
            return carry

        lax.fori_loop(0, slots // GROUP, body, 0)

    def weights(classes):
        out = jnp.zeros(classes.shape, F32)
        low, high = classes % size, classes // size
        for k in range(table_ref.shape[0]):
            table = jnp.broadcast_to(table_ref[k : k + 1, :], classes.shape)
            out = jnp.where(high == k, jnp.take_along_axis(table, low, axis=1), out)
        return out

    price[...] = price_ref[...]
    for it in range(ITERS):
        picked[...] = jnp.dot(pick, price[...].astype(BF16), preferred_element_type=F32)
        route_terms(it == 0)
        route_buf[it, me_l] = jnp.where(row_used, term[...], 0.0)
        sends = to_link(route_buf.at[it], route_send.at[it], route_recv.at[it])
        for copy in sends:
            copy.start()
        pending += sends
        if it == 0:
            def own(s, carry):
                f = flow_smem[0, s]
                own_class[pl.ds(s, 1), :] = class_ref[pl.ds(f, 1), :]
                own_access[pl.ds(s, 1), :] = access_ref[pl.ds(f, 1), :]
                return carry

            lax.fori_loop(0, slots, own, 0, unroll=8)
            own_weight = weights(own_class[...])
            for k, source in enumerate(link_sources):
                arrived(flow_all, idx_send.at[0], flow_recv, k, source, "link")
            flow_col = column(flow_ref[...])
            for d in range(n_link):
                same = (flow_col == flow_all[d, 0:1, :].astype(F32)).astype(BF16)
                match[d, :, :slots] = same
                match[d, :, slots:] = same

        route = jnp.zeros((slots, size), F32)
        for k, source in enumerate([me_l] + link_sources):
            if k:
                arrived(route_buf.at[it], route_send.at[it], route_recv.at[it], k - 1, source, "link")
            high, low = halves(route_buf[it, source])
            both = jnp.concatenate([high, low], axis=0)
            if it == ITERS - 1:
                parts[source] = both
            route = route + jnp.dot(match[source], both, preferred_element_type=F32)
        rate_b[...] = (own_weight / (own_access[...] + route)).astype(BF16)
        load_terms()
        load_buf[it, me_f] = jnp.where(row_used, term[...], 0.0)
        sends = to_flow(load_buf.at[it], load_send.at[it], load_recv.at[it])
        for copy in sends:
            copy.start()
        pending += sends
        if it == 0:
            for k, source in enumerate(flow_sources):
                arrived(link_all, idx_send.at[1], link_recv, k, source, "flow")
        if it == ITERS - 1:
            def rows(r, carry):
                at = pl.multiple_of(r * size, size)
                number = iota((size, slots), 0) + at
                route = jnp.zeros((size, size), F32)
                for d in range(n_link):
                    same = (number == flow_all[d, 0:1, :]).astype(F32).astype(BF16)
                    route = route + jnp.dot(
                        jnp.concatenate([same, same], axis=1), parts[d], preferred_element_type=F32
                    )
                block = pl.ds(at, size)
                rate_out[block, :] = weights(class_ref[block, :]) / (access_ref[block, :] + route)
                return carry

            lax.fori_loop(0, flow_blocks // size, rows, 0)

        load = jnp.zeros((link_blocks, size), F32)
        block_row = iota((link_blocks, slots), 0)
        for k, source in enumerate([me_f] + flow_sources):
            if k:
                arrived(load_buf.at[it], load_send.at[it], load_recv.at[it], k - 1, source, "flow")
            high, low = halves(load_buf[it, source])
            same = (block_row == link_all[source, 0:1, :]).astype(F32).astype(BF16)
            load = load + jnp.dot(
                jnp.concatenate([same, same], axis=1),
                jnp.concatenate([high, low], axis=0),
                preferred_element_type=F32,
            )
        new = price[...] * jnp.exp(STEP * (load / cap_ref[...] - 1.0))
        if it == ITERS - 1:
            price_out[...] = new
        else:
            price[...] = new
    for copy in pending:
        copy.wait_send()


def on_device(n_flow, n_link, route_tiles, tile_count, tile_flow, tile_link, flow_class, class_weight, access_price,
              capacity, init_price):
    slots, _, size = route_tiles.shape
    flow_blocks, link_blocks = access_price.shape[0] // size, capacity.shape[0] // size
    vmem = pl.BlockSpec(memory_space=pltpu.VMEM)
    smem = pl.BlockSpec(memory_space=pltpu.SMEM)
    dma = pltpu.SemaphoreType.DMA
    peers = max(n_flow, n_link)
    rate, price = pl.pallas_call(
        functools.partial(kernel, n_flow, n_link),
        out_shape=(
            jax.ShapeDtypeStruct((flow_blocks, size), F32),
            jax.ShapeDtypeStruct((link_blocks, size), F32),
        ),
        in_specs=[pl.BlockSpec(memory_space=pl.ANY), smem, smem] + [vmem] * 7,
        out_specs=(vmem, vmem),
        scratch_shapes=[
            pltpu.VMEM((slots, size, size), BF16),
            pltpu.VMEM((n_link, 8, slots), jnp.int32),
            pltpu.VMEM((n_flow, 8, slots), jnp.int32),
            pltpu.VMEM((ITERS, n_link, slots, size), F32),
            pltpu.VMEM((ITERS, n_flow, slots, size), F32),
            pltpu.VMEM((slots, size), F32),
            pltpu.VMEM((slots, size), F32),
            pltpu.VMEM((slots, size), BF16),
            pltpu.VMEM((n_link, slots, 2 * slots), BF16),
            pltpu.VMEM((n_link, 2 * slots, size), BF16),
            pltpu.VMEM((slots, size), jnp.int32),
            pltpu.VMEM((slots, size), F32),
            pltpu.VMEM((link_blocks, size), F32),
            dma((4,)),
            dma((2, peers)),
            dma((n_link,)),
            dma((n_flow,)),
            dma((ITERS, n_link)),
            dma((ITERS, n_link)),
            dma((ITERS, n_flow)),
            dma((ITERS, n_flow)),
        ],
        compiler_params=pltpu.CompilerParams(
            collective_id=0, has_side_effects=True, vmem_limit_bytes=48 * 1024 * 1024
        ),
    )(
        route_tiles, tile_count, tile_flow, tile_flow, tile_link,
        flow_class.reshape(flow_blocks, size), class_weight.reshape(-1, size),
        access_price.reshape(flow_blocks, size), capacity.reshape(link_blocks, size),
        init_price.reshape(link_blocks, size),
    )
    return rate.reshape(-1), price.reshape(-1)


def solution(mesh):
    return jax.shard_map(
        functools.partial(on_device, mesh.shape["flow"], mesh.shape["link"]),
        mesh=mesh,
        in_specs=(
            P("flow", "link", None),
            P("flow", "link"),
            P("flow", "link"),
            P("flow", "link"),
            P("flow"),
            P(),
            P("flow"),
            P("link"),
            P("link"),
        ),
        out_specs=(P("flow"), P("link")),
        check_vma=False,
    )
```

```python
import functools

import jax
import jax.numpy as jnp
from jax import lax
from jax.experimental import pallas as pl
from jax.experimental.pallas import tpu as pltpu
from jax.sharding import PartitionSpec as P

ITERS = 2
STEP = 0.5
GROUP = 16
F32, BF16 = jnp.float32, jnp.bfloat16


def iota(shape, dim):
    return lax.broadcasted_iota(jnp.int32, shape, dim)


def halves(x):
    high = x.astype(BF16)
    low = (x - high.astype(F32)).astype(BF16)
    return high, low


def kernel(
    n_flow, n_link,
    tiles_hbm, count_ref, flow_smem, flow_hbm, link_hbm, class_hbm, table_hbm, access_hbm, cap_hbm, price_hbm,
    rate_out, price_out,
    tiles, flow_all, link_all, route_buf, load_buf, picked, term, rate_b, match, parts, own_class, own_access, price,
    flow_ref, link_ref, class_ref, table_ref, access_ref, cap_ref,
    tile_sem, in_sem, idx_send, flow_recv, link_recv, route_send, route_recv, load_send, load_recv,
):
    slots, size = tiles.shape[0], tiles.shape[1]
    link_blocks, flow_blocks = price.shape[0], access_ref.shape[0]
    me_f, me_l = lax.axis_index("flow"), lax.axis_index("link")
    barrier = pltpu.get_barrier_semaphore()
    link_peers = [lax.rem(me_l + k, n_link) for k in range(1, n_link)]
    flow_peers = [lax.rem(me_f + k, n_flow) for k in range(1, n_flow)]
    for peer in link_peers:
        pl.semaphore_signal(barrier, inc=1, device_id={"link": peer})
    for peer in flow_peers:
        pl.semaphore_signal(barrier, inc=1, device_id={"flow": peer})

    inputs = [
        pltpu.make_async_copy(source, target, in_sem.at[k])
        for k, (source, target) in enumerate(
            [(flow_hbm, flow_ref), (link_hbm, link_ref), (price_hbm, price), (class_hbm, class_ref),
             (access_hbm, access_ref), (table_hbm, table_ref), (cap_hbm, cap_ref)]
        )
    ]
    for copy in inputs[:3]:
        copy.start()
    chunk = slots // tile_sem.shape[0]
    loads = []
    for c in range(tile_sem.shape[0]):
        copy = pltpu.make_async_copy(
            tiles_hbm.at[pl.ds(c * chunk, chunk)], tiles.at[pl.ds(c * chunk, chunk)], tile_sem.at[c]
        )
        copy.start()
        loads.append(copy)

    for copy in inputs[3:]:
        copy.start()
    for copy in inputs[:2]:
        copy.wait()
    count = count_ref[0, 0]
    used = iota((8, slots), 1) < count
    flow_all[me_l] = jnp.where(used, jnp.broadcast_to(flow_ref[...], (8, slots)), -1)
    link_all[me_f] = jnp.where(used, jnp.broadcast_to(link_ref[...], (8, slots)), -1)
    pl.semaphore_wait(barrier, n_link + n_flow - 2)

    def to_link(buf, send, recv):
        return [
            pltpu.make_async_remote_copy(
                src_ref=buf.at[me_l], dst_ref=buf.at[me_l], send_sem=send.at[k], recv_sem=recv.at[me_l],
                device_id={"link": peer}, device_id_type=pl.DeviceIdType.MESH,
            )
            for k, peer in enumerate(link_peers)
        ]

    def to_flow(buf, send, recv):
        return [
            pltpu.make_async_remote_copy(
                src_ref=buf.at[me_f], dst_ref=buf.at[me_f], send_sem=send.at[k], recv_sem=recv.at[me_f],
                device_id={"flow": peer}, device_id_type=pl.DeviceIdType.MESH,
            )
            for k, peer in enumerate(flow_peers)
        ]

    def arrived(buf, send, recv, k, source, axis):
        pltpu.make_async_remote_copy(
            src_ref=buf.at[source], dst_ref=buf.at[source], send_sem=send.at[k], recv_sem=recv.at[source],
            device_id={axis: source}, device_id_type=pl.DeviceIdType.MESH,
        ).wait_recv()

    link_sources = [lax.rem(me_l + n_link - k, n_link) for k in range(1, n_link)]
    flow_sources = [lax.rem(me_f + n_flow - k, n_flow) for k in range(1, n_flow)]
    pending = to_link(flow_all, idx_send.at[0], flow_recv) + to_flow(link_all, idx_send.at[1], link_recv)
    for copy in pending:
        copy.start()

    def column(row):
        return jnp.broadcast_to(row.astype(F32), (slots, slots)).T

    lane = iota((slots, slots), 1)
    link_col = column(link_ref[...])
    pick = jnp.concatenate(
        [(link_col == (lane + k * slots).astype(F32)).astype(BF16) for k in range(link_blocks // slots)], axis=1
    )
    row_used = iota((slots, size), 0) < count
    group_row = iota((GROUP, size), 0)

    def route_terms(first):
        def body(g, carry):
            at = pl.multiple_of(g * GROUP, GROUP)
            p = picked[pl.ds(at, GROUP), :]
            left = jnp.concatenate(
                [jnp.where(group_row == k, p, jnp.zeros_like(p)).astype(BF16) for k in range(GROUP)], axis=1
            )
            right = tiles[pl.ds(at, GROUP)].reshape(GROUP * size, size)
            term[pl.ds(at, GROUP), :] = jnp.dot(left, right, preferred_element_type=F32)
            return carry

        if first:
            per = chunk // GROUP
            for c, copy in enumerate(loads):
                copy.wait()
                lax.fori_loop(c * per, (c + 1) * per, body, 0)
        else:
            lax.fori_loop(0, slots // GROUP, body, 0)

    def load_terms():
        def body(g, carry):
            at = pl.multiple_of(g * GROUP, GROUP)
            q = rate_b[pl.ds(at, GROUP), :]
            right = tiles[pl.ds(at, GROUP)].reshape(GROUP * size, size)
            full = lax.dot_general(q, right, (((1,), (1,)), ((), ())), preferred_element_type=F32)
            total = jnp.zeros((GROUP, size), F32)
            for k in range(GROUP):
                total = jnp.where(group_row == k, full[:, k * size : (k + 1) * size], total)
            term[pl.ds(at, GROUP), :] = total
            return carry

        lax.fori_loop(0, slots // GROUP, body, 0)

    def encode(buf, it, slot):
        x = jnp.where(row_used, term[...], 0.0)
        level = jnp.ceil(jnp.log2(jnp.maximum(jnp.max(x, axis=0, keepdims=True), 1e-30)) * 8.0)
        y = jnp.sqrt(x * jnp.exp2(level * -0.125)) * 65535.0 - 32768.0
        code = jnp.clip(jnp.round(y), -32768.0, 32767.0).astype(jnp.int32)
        buf[it, slot, :slots, :] = code.astype(jnp.int16)
        buf[it, slot, slots:, :] = jnp.broadcast_to(level.astype(jnp.int32), (GROUP, size)).astype(jnp.int16)

    def decode(buf, it, slot):
        y = (buf[it, slot, :slots, :].astype(jnp.int32).astype(F32) + 32768.0) * (1.0 / 65535.0)
        level = buf[it, slot, slots:, :].astype(jnp.int32).astype(F32)[:1, :]
        return y * y * jnp.exp2(level * 0.125)

    def weights(classes):
        out = jnp.zeros(classes.shape, F32)
        low, high = classes % size, classes // size
        for k in range(table_ref.shape[0]):
            table = jnp.broadcast_to(table_ref[k : k + 1, :], classes.shape)
            out = jnp.where(high == k, jnp.take_along_axis(table, low, axis=1), out)
        return out

    inputs[2].wait()
    for it in range(ITERS):
        picked[...] = jnp.dot(pick, price[...].astype(BF16), preferred_element_type=F32)
        route_terms(it == 0)
        encode(route_buf, it, me_l)
        sends = to_link(route_buf.at[it], route_send.at[it], route_recv.at[it])
        for copy in sends:
            copy.start()
        pending += sends
        if it == 0:
            for copy in inputs[3:]:
                copy.wait()

            def own(s, carry):
                f = flow_smem[0, s]
                own_class[pl.ds(s, 1), :] = class_ref[pl.ds(f, 1), :]
                own_access[pl.ds(s, 1), :] = access_ref[pl.ds(f, 1), :]
                return carry

            lax.fori_loop(0, slots, own, 0, unroll=8)
            own_weight = weights(own_class[...])
            for k, source in enumerate(link_sources):
                arrived(flow_all, idx_send.at[0], flow_recv, k, source, "link")
            flow_col = column(flow_ref[...])
            for d in range(n_link):
                same = (flow_col == flow_all[d, 0:1, :].astype(F32)).astype(BF16)
                match[d, :, :slots] = same
                match[d, :, slots:] = same

        route = jnp.zeros((slots, size), F32)
        for k, source in enumerate([me_l] + link_sources):
            if k:
                arrived(route_buf.at[it], route_send.at[it], route_recv.at[it], k - 1, source, "link")
            high, low = halves(decode(route_buf, it, source))
            both = jnp.concatenate([high, low], axis=0)
            if it == ITERS - 1:
                parts[source] = both
            route = route + jnp.dot(match[source], both, preferred_element_type=F32)
        rate_b[...] = (own_weight / (own_access[...] + route)).astype(BF16)
        load_terms()
        encode(load_buf, it, me_f)
        sends = to_flow(load_buf.at[it], load_send.at[it], load_recv.at[it])
        for copy in sends:
            copy.start()
        pending += sends
        if it == 0:
            for k, source in enumerate(flow_sources):
                arrived(link_all, idx_send.at[1], link_recv, k, source, "flow")
        if it == ITERS - 1:
            def rows(r, carry):
                at = pl.multiple_of(r * size, size)
                number = iota((size, slots), 0) + at
                route = jnp.zeros((size, size), F32)
                for d in range(n_link):
                    same = (number == flow_all[d, 0:1, :]).astype(F32).astype(BF16)
                    route = route + jnp.dot(
                        jnp.concatenate([same, same], axis=1), parts[d], preferred_element_type=F32
                    )
                block = pl.ds(at, size)
                rate_out[block, :] = weights(class_ref[block, :]) / (access_ref[block, :] + route)
                return carry

            lax.fori_loop(0, flow_blocks // size, rows, 0)

        load = jnp.zeros((link_blocks, size), F32)
        block_row = iota((link_blocks, slots), 0)
        for k, source in enumerate([me_f] + flow_sources):
            if k:
                arrived(load_buf.at[it], load_send.at[it], load_recv.at[it], k - 1, source, "flow")
            high, low = halves(decode(load_buf, it, source))
            same = (block_row == link_all[source, 0:1, :]).astype(F32).astype(BF16)
            load = load + jnp.dot(
                jnp.concatenate([same, same], axis=1),
                jnp.concatenate([high, low], axis=0),
                preferred_element_type=F32,
            )
        new = price[...] * jnp.exp(STEP * (load / cap_ref[...] - 1.0))
        if it == ITERS - 1:
            price_out[...] = new
        else:
            price[...] = new
    for copy in pending:
        copy.wait_send()


def on_device(n_flow, n_link, route_tiles, tile_count, tile_flow, tile_link, flow_class, class_weight, access_price,
              capacity, init_price):
    slots, _, size = route_tiles.shape
    flow_blocks, link_blocks = access_price.shape[0] // size, capacity.shape[0] // size
    vmem = pl.BlockSpec(memory_space=pltpu.VMEM)
    hbm = pl.BlockSpec(memory_space=pltpu.HBM)
    smem = pl.BlockSpec(memory_space=pltpu.SMEM)
    dma = pltpu.SemaphoreType.DMA
    peers = max(n_flow, n_link)
    rate, price = pl.pallas_call(
        functools.partial(kernel, n_flow, n_link),
        out_shape=(
            jax.ShapeDtypeStruct((flow_blocks, size), F32),
            jax.ShapeDtypeStruct((link_blocks, size), F32),
        ),
        in_specs=[hbm, smem, smem] + [hbm] * 7,
        out_specs=(vmem, vmem),
        scratch_shapes=[
            pltpu.VMEM((slots, size, size), BF16),
            pltpu.VMEM((n_link, 8, slots), jnp.int32),
            pltpu.VMEM((n_flow, 8, slots), jnp.int32),
            pltpu.VMEM((ITERS, n_link, slots + GROUP, size), jnp.int16),
            pltpu.VMEM((ITERS, n_flow, slots + GROUP, size), jnp.int16),
            pltpu.VMEM((slots, size), F32),
            pltpu.VMEM((slots, size), F32),
            pltpu.VMEM((slots, size), BF16),
            pltpu.VMEM((n_link, slots, 2 * slots), BF16),
            pltpu.VMEM((n_link, 2 * slots, size), BF16),
            pltpu.VMEM((slots, size), jnp.int32),
            pltpu.VMEM((slots, size), F32),
            pltpu.VMEM((link_blocks, size), F32),
            pltpu.VMEM((1, slots), jnp.int32),
            pltpu.VMEM((1, slots), jnp.int32),
            pltpu.VMEM((flow_blocks, size), jnp.int32),
            pltpu.VMEM((class_weight.shape[0] // size, size), F32),
            pltpu.VMEM((flow_blocks, size), F32),
            pltpu.VMEM((link_blocks, size), F32),
            dma((4,)),
            dma((7,)),
            dma((2, peers)),
            dma((n_link,)),
            dma((n_flow,)),
            dma((ITERS, n_link)),
            dma((ITERS, n_link)),
            dma((ITERS, n_flow)),
            dma((ITERS, n_flow)),
        ],
        compiler_params=pltpu.CompilerParams(
            collective_id=0, has_side_effects=True, vmem_limit_bytes=60 * 1024 * 1024
        ),
    )(
        route_tiles, tile_count, tile_flow, tile_flow, tile_link,
        flow_class.reshape(flow_blocks, size), class_weight.reshape(-1, size),
        access_price.reshape(flow_blocks, size), capacity.reshape(link_blocks, size),
        init_price.reshape(link_blocks, size),
    )
    return rate.reshape(-1), price.reshape(-1)


def solution(mesh):
    return jax.shard_map(
        functools.partial(on_device, mesh.shape["flow"], mesh.shape["link"]),
        mesh=mesh,
        in_specs=(
            P("flow", "link", None),
            P("flow", "link"),
            P("flow", "link"),
            P("flow", "link"),
            P("flow"),
            P(),
            P("flow"),
            P("link"),
            P("link"),
        ),
        out_specs=(P("flow"), P("link")),
        check_vma=False,
    )
```

```python
import functools

import jax
import jax.numpy as jnp
from jax import lax
from jax.experimental import pallas as pl
from jax.experimental.pallas import tpu as pltpu
from jax.sharding import PartitionSpec as P

ITERS = 2
STEP = 0.5
GROUP = 16
HALVES = 2
F32, BF16 = jnp.float32, jnp.bfloat16


def iota(shape, dim):
    return lax.broadcasted_iota(jnp.int32, shape, dim)


def halves(x):
    high = x.astype(BF16)
    low = (x - high.astype(F32)).astype(BF16)
    return high, low


def kernel(
    n_flow, n_link,
    tiles_hbm, count_ref, flow_smem, flow_hbm, link_hbm, class_hbm, table_hbm, access_hbm, cap_hbm, price_hbm,
    rate_out, price_out,
    tiles, flow_all, link_all, route_buf, load_buf, picked, term, rate_b, match, spread, parts, own_class, own_access, price,
    flow_ref, link_ref, class_ref, table_ref, access_ref, cap_ref,
    tile_sem, in_sem, idx_send, flow_recv, link_recv, route_send, route_recv, load_send, load_recv,
):
    slots, size = tiles.shape[0], tiles.shape[1]
    link_blocks, flow_blocks = price.shape[0], access_ref.shape[0]
    me_f, me_l = lax.axis_index("flow"), lax.axis_index("link")
    barrier = pltpu.get_barrier_semaphore()
    link_peers = [lax.rem(me_l + k, n_link) for k in range(1, n_link)]
    flow_peers = [lax.rem(me_f + k, n_flow) for k in range(1, n_flow)]
    for peer in link_peers:
        pl.semaphore_signal(barrier, inc=1, device_id={"link": peer})
    for peer in flow_peers:
        pl.semaphore_signal(barrier, inc=1, device_id={"flow": peer})

    inputs = [
        pltpu.make_async_copy(source, target, in_sem.at[k])
        for k, (source, target) in enumerate(
            [(flow_hbm, flow_ref), (link_hbm, link_ref), (price_hbm, price), (class_hbm, class_ref),
             (access_hbm, access_ref), (table_hbm, table_ref), (cap_hbm, cap_ref)]
        )
    ]
    for copy in inputs[:3]:
        copy.start()
    chunk = slots // tile_sem.shape[0]
    loads = []
    for c in range(tile_sem.shape[0]):
        copy = pltpu.make_async_copy(
            tiles_hbm.at[pl.ds(c * chunk, chunk)], tiles.at[pl.ds(c * chunk, chunk)], tile_sem.at[c]
        )
        copy.start()
        loads.append(copy)

    for copy in inputs[3:]:
        copy.start()
    for copy in inputs[:2]:
        copy.wait()
    count = count_ref[0, 0]
    used = iota((8, slots), 1) < count
    flow_all[me_l] = jnp.where(used, jnp.broadcast_to(flow_ref[...], (8, slots)), -1)
    link_all[me_f] = jnp.where(used, jnp.broadcast_to(link_ref[...], (8, slots)), -1)
    pl.semaphore_wait(barrier, n_link + n_flow - 2)

    def to_link(buf, send, recv):
        return [
            pltpu.make_async_remote_copy(
                src_ref=buf.at[me_l], dst_ref=buf.at[me_l], send_sem=send.at[k], recv_sem=recv.at[me_l],
                device_id={"link": peer}, device_id_type=pl.DeviceIdType.MESH,
            )
            for k, peer in enumerate(link_peers)
        ]

    def to_flow(buf, send, recv):
        return [
            pltpu.make_async_remote_copy(
                src_ref=buf.at[me_f], dst_ref=buf.at[me_f], send_sem=send.at[k], recv_sem=recv.at[me_f],
                device_id={"flow": peer}, device_id_type=pl.DeviceIdType.MESH,
            )
            for k, peer in enumerate(flow_peers)
        ]

    def copy_of(buf, index, send, recv, k, target, axis):
        return pltpu.make_async_remote_copy(
            src_ref=buf.at[index], dst_ref=buf.at[index], send_sem=send.at[k], recv_sem=recv.at[index],
            device_id={axis: target}, device_id_type=pl.DeviceIdType.MESH,
        )

    def arrived(buf, send, recv, k, source, axis):
        pltpu.make_async_remote_copy(
            src_ref=buf.at[source], dst_ref=buf.at[source], send_sem=send.at[k], recv_sem=recv.at[source],
            device_id={axis: source}, device_id_type=pl.DeviceIdType.MESH,
        ).wait_recv()

    link_sources = [lax.rem(me_l + n_link - k, n_link) for k in range(1, n_link)]
    partner = me_l + 1 - 2 * lax.rem(me_l, 2)
    steps = sorted(range(1, n_link // 2), key=lambda k: min(k, n_link // 2 - k))
    line = [lax.rem(me_l + 2 * k, n_link) for k in steps]
    partner_line = [lax.rem(partner + 2 * k, n_link) for k in steps]
    flow_sources = [lax.rem(me_f + n_flow - k, n_flow) for k in range(1, n_flow)]
    pending = to_link(flow_all, idx_send.at[0], flow_recv) + to_flow(link_all, idx_send.at[1], link_recv)
    for copy in pending:
        copy.start()

    def column(row):
        return jnp.broadcast_to(row.astype(F32), (slots, slots)).T

    lane = iota((slots, slots), 1)
    link_col = column(link_ref[...])
    pick = jnp.concatenate(
        [(link_col == (lane + k * slots).astype(F32)).astype(BF16) for k in range(link_blocks // slots)], axis=1
    )
    row_used = iota((slots, size), 0) < count
    group_row = iota((GROUP, size), 0)

    def route_terms(first, half):
        def body(g, carry):
            at = pl.multiple_of(g * GROUP, GROUP)
            p = picked[pl.ds(at, GROUP), :]
            left = jnp.concatenate(
                [jnp.where(group_row == k, p, jnp.zeros_like(p)).astype(BF16) for k in range(GROUP)], axis=1
            )
            right = tiles[pl.ds(at, GROUP)].reshape(GROUP * size, size)
            term[pl.ds(at, GROUP), :] = jnp.dot(left, right, preferred_element_type=F32)
            return carry

        per = slots // HALVES // GROUP
        if first:
            for copy in loads[half * len(loads) // HALVES : (half + 1) * len(loads) // HALVES]:
                copy.wait()
        lax.fori_loop(half * per, (half + 1) * per, body, 0)

    def load_terms(half):
        def body(g, carry):
            at = pl.multiple_of(g * GROUP, GROUP)
            q = rate_b[pl.ds(at, GROUP), :]
            right = tiles[pl.ds(at, GROUP)].reshape(GROUP * size, size)
            full = lax.dot_general(q, right, (((1,), (1,)), ((), ())), preferred_element_type=F32)
            total = jnp.zeros((GROUP, size), F32)
            for k in range(GROUP):
                total = jnp.where(group_row == k, full[:, k * size : (k + 1) * size], total)
            term[pl.ds(at, GROUP), :] = total
            return carry

        per = slots // HALVES // GROUP
        lax.fori_loop(half * per, (half + 1) * per, body, 0)

    part = slots // HALVES

    def encode(buf, it, half, slot):
        at = half * part
        x = jnp.where(row_used[at : at + part], term[at : at + part, :], 0.0)
        level = jnp.ceil(jnp.log2(jnp.maximum(jnp.max(x, axis=0, keepdims=True), 1e-30)) * 8.0)
        y = jnp.sqrt(x * jnp.exp2(level * -0.125)) * 65535.0 - 32768.0
        code = jnp.clip(jnp.round(y), -32768.0, 32767.0).astype(jnp.int32)
        buf[it, half, slot, :part, :] = code.astype(jnp.int16)
        buf[it, half, slot, part:, :] = jnp.broadcast_to(level.astype(jnp.int32), (GROUP, size)).astype(jnp.int16)

    def decode(buf, it, slot):
        found = []
        for half in range(HALVES):
            y = (buf[it, half, slot, :part, :].astype(jnp.int32).astype(F32) + 32768.0) * (1.0 / 65535.0)
            level = buf[it, half, slot, part:, :].astype(jnp.int32).astype(F32)[:1, :]
            found.append(y * y * jnp.exp2(level * 0.125))
        return jnp.concatenate(found, axis=0)

    def weights(classes):
        out = jnp.zeros(classes.shape, F32)
        low, high = classes % size, classes // size
        for k in range(table_ref.shape[0]):
            table = jnp.broadcast_to(table_ref[k : k + 1, :], classes.shape)
            out = jnp.where(high == k, jnp.take_along_axis(table, low, axis=1), out)
        return out

    inputs[2].wait()
    for it in range(ITERS):
        picked[...] = jnp.dot(pick, price[...].astype(BF16), preferred_element_type=F32)
        for half in range(HALVES):
            route_terms(it == 0, half)
            encode(route_buf, it, half, me_l)
            for k, peer in enumerate(line + [partner]):
                copy = copy_of(route_buf.at[it, half], me_l, route_send.at[it, half], route_recv.at[it, half], k, peer, "link")
                copy.start()
                pending.append(copy)
        if it == 0:
            for copy in inputs[3:]:
                copy.wait()

            def own(s, carry):
                f = flow_smem[0, s]
                own_class[pl.ds(s, 1), :] = class_ref[pl.ds(f, 1), :]
                own_access[pl.ds(s, 1), :] = access_ref[pl.ds(f, 1), :]
                return carry

            lax.fori_loop(0, slots, own, 0, unroll=8)
            own_weight = weights(own_class[...])
            for k, source in enumerate(link_sources):
                arrived(flow_all, idx_send.at[0], flow_recv, k, source, "link")
            flow_col = column(flow_ref[...])
            for d in range(n_link):
                same = (flow_col == flow_all[d, 0:1, :].astype(F32)).astype(BF16)
                match[d, :, :slots] = same
                match[d, :, slots:] = same

        route = jnp.zeros((slots, size), F32)
        def add(source, route):
            high, low = halves(decode(route_buf, it, source))
            both = jnp.concatenate([high, low], axis=0)
            if it == ITERS - 1:
                parts[source] = both
            return route + jnp.dot(match[source], both, preferred_element_type=F32)

        def await_route(half, source):
            copy_of(
                route_buf.at[it, half], source, route_send.at[it, half], route_recv.at[it, half], 0, partner, "link"
            ).wait_recv()

        route = add(me_l, route)
        for half in range(HALVES):
            for k, source in enumerate(line):
                await_route(half, source)
                copy = copy_of(
                    route_buf.at[it, half], source, route_send.at[it, half], route_recv.at[it, half],
                    n_link // 2 + k, partner, "link",
                )
                copy.start()
                pending.append(copy)
        for source in line:
            route = add(source, route)
        for source in [partner] + partner_line:
            for half in range(HALVES):
                await_route(half, source)
            route = add(source, route)
        rate_b[...] = (own_weight / (own_access[...] + route)).astype(BF16)
        for half in range(HALVES):
            load_terms(half)
            encode(load_buf, it, half, me_f)
            for k, peer in enumerate(flow_peers):
                copy = copy_of(load_buf.at[it, half], me_f, load_send.at[it, half], load_recv.at[it, half], k, peer, "flow")
                copy.start()
                pending.append(copy)
        if it == 0:
            for k, source in enumerate(flow_sources):
                arrived(link_all, idx_send.at[1], link_recv, k, source, "flow")
            block_row = iota((link_blocks, slots), 0)
            for d in range(n_flow):
                same = (block_row == link_all[d, 0:1, :]).astype(F32).astype(BF16)
                spread[d, :, :slots] = same
                spread[d, :, slots:] = same
        if it == ITERS - 1:
            def rows(r, carry):
                at = pl.multiple_of(r * size, size)
                number = iota((size, slots), 0) + at
                route = jnp.zeros((size, size), F32)
                for d in range(n_link):
                    same = (number == flow_all[d, 0:1, :]).astype(F32).astype(BF16)
                    route = route + jnp.dot(
                        jnp.concatenate([same, same], axis=1), parts[d], preferred_element_type=F32
                    )
                block = pl.ds(at, size)
                rate_out[block, :] = weights(class_ref[block, :]) / (access_ref[block, :] + route)
                return carry

            lax.fori_loop(0, flow_blocks // size, rows, 0)

        load = jnp.zeros((link_blocks, size), F32)
        for k, source in enumerate([me_f] + flow_sources):
            if k:
                for half in range(HALVES):
                    copy_of(
                        load_buf.at[it, half], source, load_send.at[it, half], load_recv.at[it, half], 0, source, "flow"
                    ).wait_recv()
            high, low = halves(decode(load_buf, it, source))
            load = load + jnp.dot(
                spread[source], jnp.concatenate([high, low], axis=0), preferred_element_type=F32
            )
        new = price[...] * jnp.exp(STEP * (load / cap_ref[...] - 1.0))
        if it == ITERS - 1:
            price_out[...] = new
        else:
            price[...] = new
    for copy in pending:
        copy.wait_send()


def on_device(n_flow, n_link, route_tiles, tile_count, tile_flow, tile_link, flow_class, class_weight, access_price,
              capacity, init_price):
    slots, _, size = route_tiles.shape
    flow_blocks, link_blocks = access_price.shape[0] // size, capacity.shape[0] // size
    vmem = pl.BlockSpec(memory_space=pltpu.VMEM)
    hbm = pl.BlockSpec(memory_space=pltpu.HBM)
    smem = pl.BlockSpec(memory_space=pltpu.SMEM)
    dma = pltpu.SemaphoreType.DMA
    peers = max(n_flow, n_link)
    rate, price = pl.pallas_call(
        functools.partial(kernel, n_flow, n_link),
        out_shape=(
            jax.ShapeDtypeStruct((flow_blocks, size), F32),
            jax.ShapeDtypeStruct((link_blocks, size), F32),
        ),
        in_specs=[hbm, smem, smem] + [hbm] * 7,
        out_specs=(vmem, vmem),
        scratch_shapes=[
            pltpu.VMEM((slots, size, size), BF16),
            pltpu.VMEM((n_link, 8, slots), jnp.int32),
            pltpu.VMEM((n_flow, 8, slots), jnp.int32),
            pltpu.VMEM((ITERS, HALVES, n_link, slots // HALVES + GROUP, size), jnp.int16),
            pltpu.VMEM((ITERS, HALVES, n_flow, slots // HALVES + GROUP, size), jnp.int16),
            pltpu.VMEM((slots, size), F32),
            pltpu.VMEM((slots, size), F32),
            pltpu.VMEM((slots, size), BF16),
            pltpu.VMEM((n_link, slots, 2 * slots), BF16),
            pltpu.VMEM((n_flow, link_blocks, 2 * slots), BF16),
            pltpu.VMEM((n_link, 2 * slots, size), BF16),
            pltpu.VMEM((slots, size), jnp.int32),
            pltpu.VMEM((slots, size), F32),
            pltpu.VMEM((link_blocks, size), F32),
            pltpu.VMEM((1, slots), jnp.int32),
            pltpu.VMEM((1, slots), jnp.int32),
            pltpu.VMEM((flow_blocks, size), jnp.int32),
            pltpu.VMEM((class_weight.shape[0] // size, size), F32),
            pltpu.VMEM((flow_blocks, size), F32),
            pltpu.VMEM((link_blocks, size), F32),
            dma((4,)),
            dma((7,)),
            dma((2, peers)),
            dma((n_link,)),
            dma((n_flow,)),
            dma((ITERS, HALVES, n_link)),
            dma((ITERS, HALVES, n_link)),
            dma((ITERS, HALVES, n_flow)),
            dma((ITERS, HALVES, n_flow)),
        ],
        compiler_params=pltpu.CompilerParams(
            collective_id=0, has_side_effects=True, vmem_limit_bytes=60 * 1024 * 1024
        ),
    )(
        route_tiles, tile_count, tile_flow, tile_flow, tile_link,
        flow_class.reshape(flow_blocks, size), class_weight.reshape(-1, size),
        access_price.reshape(flow_blocks, size), capacity.reshape(link_blocks, size),
        init_price.reshape(link_blocks, size),
    )
    return rate.reshape(-1), price.reshape(-1)


def solution(mesh):
    return jax.shard_map(
        functools.partial(on_device, mesh.shape["flow"], mesh.shape["link"]),
        mesh=mesh,
        in_specs=(
            P("flow", "link", None),
            P("flow", "link"),
            P("flow", "link"),
            P("flow", "link"),
            P("flow"),
            P(),
            P("flow"),
            P("link"),
            P("link"),
        ),
        out_specs=(P("flow"), P("link")),
        check_vma=False,
    )
```

```python
import functools

import jax
import jax.numpy as jnp
from jax import lax
from jax.experimental import pallas as pl
from jax.experimental.pallas import tpu as pltpu
from jax.sharding import PartitionSpec as P

ITERS = 2
STEP = 0.5
GROUP = 16
HALVES = 1
F32, BF16 = jnp.float32, jnp.bfloat16


def iota(shape, dim):
    return lax.broadcasted_iota(jnp.int32, shape, dim)


def halves(x):
    high = x.astype(BF16)
    low = (x - high.astype(F32)).astype(BF16)
    return high, low


def kernel(
    n_flow, n_link,
    tiles_hbm, count_ref, flow_smem, flow_hbm, link_hbm, class_hbm, table_hbm, access_hbm, cap_hbm, price_hbm,
    rate_out, price_out,
    tiles, flow_all, link_all, route_buf, load_buf, picked, term, rate_b, match, spread, parts, own_class, own_access, price,
    flow_ref, link_ref, class_ref, table_ref, access_ref, cap_ref,
    tile_sem, in_sem, route_send, route_recv, load_send, load_recv,
):
    slots, size = tiles.shape[0], tiles.shape[1]
    link_blocks, flow_blocks = price.shape[0], access_ref.shape[0]
    me_f, me_l = lax.axis_index("flow"), lax.axis_index("link")
    barrier = pltpu.get_barrier_semaphore()
    partner = me_l + 1 - 2 * lax.rem(me_l, 2)
    steps = sorted(range(1, n_link // 2), key=lambda k: min(k, n_link // 2 - k))
    line = [lax.rem(me_l + 2 * k, n_link) for k in steps]
    partner_line = [lax.rem(partner + 2 * k, n_link) for k in steps]
    flow_peers = [lax.rem(me_f + k, n_flow) for k in range(1, n_flow)]
    for peer in line + [partner]:
        pl.semaphore_signal(barrier, inc=1, device_id={"link": peer})
    for peer in flow_peers:
        pl.semaphore_signal(barrier, inc=1, device_id={"flow": peer})

    inputs = [
        pltpu.make_async_copy(source, target, in_sem.at[k])
        for k, (source, target) in enumerate(
            [(flow_hbm, flow_ref), (link_hbm, link_ref), (price_hbm, price), (class_hbm, class_ref),
             (access_hbm, access_ref), (table_hbm, table_ref), (cap_hbm, cap_ref)]
        )
    ]
    for copy in inputs[:3]:
        copy.start()
    chunk = slots // tile_sem.shape[0]
    loads = []
    for c in range(tile_sem.shape[0]):
        copy = pltpu.make_async_copy(
            tiles_hbm.at[pl.ds(c * chunk, chunk)], tiles.at[pl.ds(c * chunk, chunk)], tile_sem.at[c]
        )
        copy.start()
        loads.append(copy)

    for copy in inputs[3:]:
        copy.start()
    for copy in inputs[:2]:
        copy.wait()
    count = count_ref[0, 0]
    used = iota((8, slots), 1) < count
    flow_all[me_l] = jnp.where(used, jnp.broadcast_to(flow_ref[...], (8, slots)), -1)
    link_all[me_f] = jnp.where(used, jnp.broadcast_to(link_ref[...], (8, slots)), -1)

    def copy_of(buf, index, send, recv, k, target, axis):
        return pltpu.make_async_remote_copy(
            src_ref=buf.at[index], dst_ref=buf.at[index], send_sem=send.at[k], recv_sem=recv.at[index],
            device_id={axis: target}, device_id_type=pl.DeviceIdType.MESH,
        )

    flow_sources = [lax.rem(me_f + n_flow - k, n_flow) for k in range(1, n_flow)]
    pending = []

    def column(row):
        return jnp.broadcast_to(row.astype(F32), (slots, slots)).T

    lane = iota((slots, slots), 1)
    link_col = column(link_ref[...])
    pick = jnp.concatenate(
        [(link_col == (lane + k * slots).astype(F32)).astype(BF16) for k in range(link_blocks // slots)], axis=1
    )
    row_used = iota((slots, size), 0) < count
    group_row = iota((GROUP, size), 0)

    def route_terms(first, half):
        def body(g, carry):
            at = pl.multiple_of(g * GROUP, GROUP)
            p = picked[pl.ds(at, GROUP), :]
            left = jnp.concatenate(
                [jnp.where(group_row == k, p, jnp.zeros_like(p)).astype(BF16) for k in range(GROUP)], axis=1
            )
            right = tiles[pl.ds(at, GROUP)].reshape(GROUP * size, size)
            term[pl.ds(at, GROUP), :] = jnp.dot(left, right, preferred_element_type=F32)
            return carry

        per = slots // HALVES // GROUP
        if first:
            for copy in loads[half * len(loads) // HALVES : (half + 1) * len(loads) // HALVES]:
                copy.wait()
        lax.fori_loop(half * per, (half + 1) * per, body, 0)

    def load_terms(half):
        def body(g, carry):
            at = pl.multiple_of(g * GROUP, GROUP)
            q = rate_b[pl.ds(at, GROUP), :]
            right = tiles[pl.ds(at, GROUP)].reshape(GROUP * size, size)
            full = lax.dot_general(q, right, (((1,), (1,)), ((), ())), preferred_element_type=F32)
            total = jnp.zeros((GROUP, size), F32)
            for k in range(GROUP):
                total = jnp.where(group_row == k, full[:, k * size : (k + 1) * size], total)
            term[pl.ds(at, GROUP), :] = total
            return carry

        per = slots // HALVES // GROUP
        lax.fori_loop(half * per, (half + 1) * per, body, 0)

    part = slots // HALVES

    def encode(buf, it, half, slot, numbers):
        at = half * part
        x = jnp.where(row_used[at : at + part], term[at : at + part, :], 0.0)
        level = jnp.ceil(jnp.log2(jnp.maximum(jnp.max(x, axis=0, keepdims=True), 1e-30)) * 8.0)
        y = jnp.sqrt(x * jnp.exp2(level * -0.125)) * 65535.0 - 32768.0
        code = jnp.clip(jnp.round(y), -32768.0, 32767.0).astype(jnp.int32)
        buf[it, half, slot, :part, :] = code.astype(jnp.int16)
        buf[it, half, slot, part:, :] = jnp.where(
            group_row < GROUP // 2, level.astype(jnp.int32), numbers[slot, 0:1, :]
        ).astype(jnp.int16)

    def decode(buf, it, slot):
        found = []
        for half in range(HALVES):
            y = (buf[it, half, slot, :part, :].astype(jnp.int32).astype(F32) + 32768.0) * (1.0 / 65535.0)
            level = buf[it, half, slot, part:, :].astype(jnp.int32).astype(F32)[:1, :]
            found.append(y * y * jnp.exp2(level * 0.125))
        return jnp.concatenate(found, axis=0)

    def numbers_of(buf, it, slot):
        row = buf[it, 0, slot, part:, :].astype(jnp.int32)[GROUP // 2 :, :]
        return row[:8, :]

    def weights(classes):
        out = jnp.zeros(classes.shape, F32)
        low, high = classes % size, classes // size
        for k in range(table_ref.shape[0]):
            table = jnp.broadcast_to(table_ref[k : k + 1, :], classes.shape)
            out = jnp.where(high == k, jnp.take_along_axis(table, low, axis=1), out)
        return out

    inputs[2].wait()
    for it in range(ITERS):
        picked[...] = jnp.dot(pick, price[...].astype(BF16), preferred_element_type=F32)
        for half in range(HALVES):
            route_terms(it == 0, half)
            encode(route_buf, it, half, me_l, flow_all)
            if it == 0 and half == 0:
                pl.semaphore_wait(barrier, n_link // 2 + n_flow - 1)
            for k, peer in enumerate(line + [partner]):
                copy = copy_of(route_buf.at[it, half], me_l, route_send.at[it, half], route_recv.at[it, half], k, peer, "link")
                copy.start()
                pending.append(copy)
        if it == 0:
            for copy in inputs[3:]:
                copy.wait()

            def own(s, carry):
                f = flow_smem[0, s]
                own_class[pl.ds(s, 1), :] = class_ref[pl.ds(f, 1), :]
                own_access[pl.ds(s, 1), :] = access_ref[pl.ds(f, 1), :]
                return carry

            lax.fori_loop(0, slots, own, 0, unroll=8)
            own_weight = weights(own_class[...])
            flow_col = column(flow_ref[...])

        route = jnp.zeros((slots, size), F32)

        def add(source, route):
            if it == 0:
                row = numbers_of(route_buf, it, source)
                flow_all[source] = row
                same = (flow_col == row[0:1, :].astype(F32)).astype(BF16)
                match[source, :, :slots] = same
                match[source, :, slots:] = same
            high, low = halves(decode(route_buf, it, source))
            both = jnp.concatenate([high, low], axis=0)
            if it == ITERS - 1:
                parts[source] = both
            return route + jnp.dot(match[source], both, preferred_element_type=F32)

        def await_route(half, source):
            copy_of(
                route_buf.at[it, half], source, route_send.at[it, half], route_recv.at[it, half], 0, partner, "link"
            ).wait_recv()

        route = add(me_l, route)
        for half in range(HALVES):
            for k, source in enumerate(line):
                await_route(half, source)
                copy = copy_of(
                    route_buf.at[it, half], source, route_send.at[it, half], route_recv.at[it, half],
                    n_link // 2 + k, partner, "link",
                )
                copy.start()
                pending.append(copy)
        for source in line:
            route = add(source, route)
        for source in [partner] + partner_line:
            for half in range(HALVES):
                await_route(half, source)
            route = add(source, route)
        rate_b[...] = (own_weight / (own_access[...] + route)).astype(BF16)
        for half in range(HALVES):
            load_terms(half)
            encode(load_buf, it, half, me_f, link_all)
            for k, peer in enumerate(flow_peers):
                copy = copy_of(load_buf.at[it, half], me_f, load_send.at[it, half], load_recv.at[it, half], k, peer, "flow")
                copy.start()
                pending.append(copy)
        if it == ITERS - 1:
            def rows(r, carry):
                at = pl.multiple_of(r * size, size)
                number = iota((size, slots), 0) + at
                route = jnp.zeros((size, size), F32)
                for d in range(n_link):
                    same = (number == flow_all[d, 0:1, :]).astype(F32).astype(BF16)
                    route = route + jnp.dot(
                        jnp.concatenate([same, same], axis=1), parts[d], preferred_element_type=F32
                    )
                block = pl.ds(at, size)
                rate_out[block, :] = weights(class_ref[block, :]) / (access_ref[block, :] + route)
                return carry

            lax.fori_loop(0, flow_blocks // size, rows, 0)

        load = jnp.zeros((link_blocks, size), F32)
        for k, source in enumerate([me_f] + flow_sources):
            if k:
                for half in range(HALVES):
                    copy_of(
                        load_buf.at[it, half], source, load_send.at[it, half], load_recv.at[it, half], 0, source, "flow"
                    ).wait_recv()
            if it == 0:
                row = numbers_of(load_buf, it, source)
                same = (iota((link_blocks, slots), 0) == row[0:1, :]).astype(F32).astype(BF16)
                spread[source, :, :slots] = same
                spread[source, :, slots:] = same
            high, low = halves(decode(load_buf, it, source))
            load = load + jnp.dot(
                spread[source], jnp.concatenate([high, low], axis=0), preferred_element_type=F32
            )
        new = price[...] * jnp.exp(STEP * (load / cap_ref[...] - 1.0))
        if it == ITERS - 1:
            price_out[...] = new
        else:
            price[...] = new
    for copy in pending:
        copy.wait_send()


def on_device(n_flow, n_link, route_tiles, tile_count, tile_flow, tile_link, flow_class, class_weight, access_price,
              capacity, init_price):
    slots, _, size = route_tiles.shape
    flow_blocks, link_blocks = access_price.shape[0] // size, capacity.shape[0] // size
    vmem = pl.BlockSpec(memory_space=pltpu.VMEM)
    hbm = pl.BlockSpec(memory_space=pltpu.HBM)
    smem = pl.BlockSpec(memory_space=pltpu.SMEM)
    dma = pltpu.SemaphoreType.DMA
    rate, price = pl.pallas_call(
        functools.partial(kernel, n_flow, n_link),
        out_shape=(
            jax.ShapeDtypeStruct((flow_blocks, size), F32),
            jax.ShapeDtypeStruct((link_blocks, size), F32),
        ),
        in_specs=[hbm, smem, smem] + [hbm] * 7,
        out_specs=(vmem, vmem),
        scratch_shapes=[
            pltpu.VMEM((slots, size, size), BF16),
            pltpu.VMEM((n_link, 8, slots), jnp.int32),
            pltpu.VMEM((n_flow, 8, slots), jnp.int32),
            pltpu.VMEM((ITERS, HALVES, n_link, slots // HALVES + GROUP, size), jnp.int16),
            pltpu.VMEM((ITERS, HALVES, n_flow, slots // HALVES + GROUP, size), jnp.int16),
            pltpu.VMEM((slots, size), F32),
            pltpu.VMEM((slots, size), F32),
            pltpu.VMEM((slots, size), BF16),
            pltpu.VMEM((n_link, slots, 2 * slots), BF16),
            pltpu.VMEM((n_flow, link_blocks, 2 * slots), BF16),
            pltpu.VMEM((n_link, 2 * slots, size), BF16),
            pltpu.VMEM((slots, size), jnp.int32),
            pltpu.VMEM((slots, size), F32),
            pltpu.VMEM((link_blocks, size), F32),
            pltpu.VMEM((1, slots), jnp.int32),
            pltpu.VMEM((1, slots), jnp.int32),
            pltpu.VMEM((flow_blocks, size), jnp.int32),
            pltpu.VMEM((class_weight.shape[0] // size, size), F32),
            pltpu.VMEM((flow_blocks, size), F32),
            pltpu.VMEM((link_blocks, size), F32),
            dma((4,)),
            dma((7,)),
            dma((ITERS, HALVES, n_link)),
            dma((ITERS, HALVES, n_link)),
            dma((ITERS, HALVES, n_flow)),
            dma((ITERS, HALVES, n_flow)),
        ],
        compiler_params=pltpu.CompilerParams(
            collective_id=0, has_side_effects=True, vmem_limit_bytes=60 * 1024 * 1024
        ),
    )(
        route_tiles, tile_count, tile_flow, tile_flow, tile_link,
        flow_class.reshape(flow_blocks, size), class_weight.reshape(-1, size),
        access_price.reshape(flow_blocks, size), capacity.reshape(link_blocks, size),
        init_price.reshape(link_blocks, size),
    )
    return rate.reshape(-1), price.reshape(-1)


def solution(mesh):
    return jax.shard_map(
        functools.partial(on_device, mesh.shape["flow"], mesh.shape["link"]),
        mesh=mesh,
        in_specs=(
            P("flow", "link", None),
            P("flow", "link"),
            P("flow", "link"),
            P("flow", "link"),
            P("flow"),
            P(),
            P("flow"),
            P("link"),
            P("link"),
        ),
        out_specs=(P("flow"), P("link")),
        check_vma=False,
    )
```

```python
import functools

import jax
import jax.numpy as jnp
from jax import lax
from jax.experimental import pallas as pl
from jax.experimental.pallas import tpu as pltpu
from jax.sharding import PartitionSpec as P

ITERS = 2
STEP = 0.5
GROUP = 16
HALVES = 2
F32, BF16 = jnp.float32, jnp.bfloat16


def iota(shape, dim):
    return lax.broadcasted_iota(jnp.int32, shape, dim)


def halves(x):
    high = x.astype(BF16)
    low = (x - high.astype(F32)).astype(BF16)
    return high, low


def kernel(
    n_flow, n_link,
    tiles_hbm, count_ref, flow_smem, flow_hbm, link_hbm, class_hbm, table_hbm, access_hbm, cap_hbm, price_hbm,
    rate_out, price_out,
    tiles, flow_all, link_all, route_buf, load_buf, picked, term, rate_b, match, spread, parts, own_class, own_access, price,
    flow_ref, link_ref, class_ref, table_ref, access_ref, cap_ref,
    tile_sem, in_sem, route_send, route_recv, load_send, load_recv,
):
    slots, size = tiles.shape[0], tiles.shape[1]
    link_blocks, flow_blocks = price.shape[0], access_ref.shape[0]
    me_f, me_l = lax.axis_index("flow"), lax.axis_index("link")
    barrier = pltpu.get_barrier_semaphore()
    partner = me_l + 1 - 2 * lax.rem(me_l, 2)
    steps = sorted(range(1, n_link // 2), key=lambda k: min(k, n_link // 2 - k))
    line = [lax.rem(me_l + 2 * k, n_link) for k in steps]
    partner_line = [lax.rem(partner + 2 * k, n_link) for k in steps]
    flow_peers = [lax.rem(me_f + k, n_flow) for k in range(1, n_flow)]
    for peer in line + [partner]:
        pl.semaphore_signal(barrier, inc=1, device_id={"link": peer})
    for peer in flow_peers:
        pl.semaphore_signal(barrier, inc=1, device_id={"flow": peer})

    inputs = [
        pltpu.make_async_copy(source, target, in_sem.at[k])
        for k, (source, target) in enumerate(
            [(flow_hbm, flow_ref), (link_hbm, link_ref), (price_hbm, price), (class_hbm, class_ref),
             (access_hbm, access_ref), (table_hbm, table_ref), (cap_hbm, cap_ref)]
        )
    ]
    for copy in inputs[:3]:
        copy.start()
    chunk = slots // tile_sem.shape[0]
    loads = []
    for c in range(tile_sem.shape[0]):
        copy = pltpu.make_async_copy(
            tiles_hbm.at[pl.ds(c * chunk, chunk)], tiles.at[pl.ds(c * chunk, chunk)], tile_sem.at[c]
        )
        copy.start()
        loads.append(copy)

    for copy in inputs[3:]:
        copy.start()
    for copy in inputs[:2]:
        copy.wait()
    count = count_ref[0, 0]
    used = iota((8, slots), 1) < count
    flow_all[me_l] = jnp.where(used, jnp.broadcast_to(flow_ref[...], (8, slots)), -1)
    link_all[me_f] = jnp.where(used, jnp.broadcast_to(link_ref[...], (8, slots)), -1)

    def copy_of(buf, index, send, recv, k, target, axis):
        return pltpu.make_async_remote_copy(
            src_ref=buf.at[index], dst_ref=buf.at[index], send_sem=send.at[k], recv_sem=recv.at[index],
            device_id={axis: target}, device_id_type=pl.DeviceIdType.MESH,
        )

    flow_sources = [lax.rem(me_f + n_flow - k, n_flow) for k in range(1, n_flow)]
    pending = []

    def column(row):
        return jnp.broadcast_to(row.astype(F32), (slots, slots)).T

    lane = iota((slots, slots), 1)
    link_col = column(link_ref[...])
    pick = jnp.concatenate(
        [(link_col == (lane + k * slots).astype(F32)).astype(BF16) for k in range(link_blocks // slots)], axis=1
    )
    row_used = iota((slots, size), 0) < count
    group_row = iota((GROUP, size), 0)

    def route_terms(first, half):
        def body(g, carry):
            at = pl.multiple_of(g * GROUP, GROUP)
            p = picked[pl.ds(at, GROUP), :]
            left = jnp.concatenate(
                [jnp.where(group_row == k, p, jnp.zeros_like(p)).astype(BF16) for k in range(GROUP)], axis=1
            )
            right = tiles[pl.ds(at, GROUP)].reshape(GROUP * size, size)
            term[pl.ds(at, GROUP), :] = jnp.dot(left, right, preferred_element_type=F32)
            return carry

        per = slots // HALVES // GROUP
        if first:
            for copy in loads[half * len(loads) // HALVES : (half + 1) * len(loads) // HALVES]:
                copy.wait()
        lax.fori_loop(half * per, (half + 1) * per, body, 0)

    def load_terms(half):
        def body(g, carry):
            at = pl.multiple_of(g * GROUP, GROUP)
            q = rate_b[pl.ds(at, GROUP), :]
            right = tiles[pl.ds(at, GROUP)].reshape(GROUP * size, size)
            full = lax.dot_general(q, right, (((1,), (1,)), ((), ())), preferred_element_type=F32)
            total = jnp.zeros((GROUP, size), F32)
            for k in range(GROUP):
                total = jnp.where(group_row == k, full[:, k * size : (k + 1) * size], total)
            term[pl.ds(at, GROUP), :] = total
            return carry

        per = slots // HALVES // GROUP
        lax.fori_loop(half * per, (half + 1) * per, body, 0)

    part = slots // HALVES

    def encode(buf, it, half, slot, numbers):
        at = half * part
        x = jnp.where(row_used[at : at + part], term[at : at + part, :], 0.0)
        level = jnp.ceil(jnp.log2(jnp.maximum(jnp.max(x, axis=0, keepdims=True), 1e-30)) * 8.0)
        y = jnp.sqrt(x * jnp.exp2(level * -0.125)) * 65535.0 - 32768.0
        code = jnp.clip(jnp.round(y), -32768.0, 32767.0).astype(jnp.int32)
        buf[it, half, slot, :part, :] = code.astype(jnp.int16)
        buf[it, half, slot, part:, :] = jnp.where(
            group_row < GROUP // 2, level.astype(jnp.int32), numbers[slot, 0:1, :]
        ).astype(jnp.int16)

    def decode(buf, it, slot):
        found = []
        for half in range(HALVES):
            y = (buf[it, half, slot, :part, :].astype(jnp.int32).astype(F32) + 32768.0) * (1.0 / 65535.0)
            level = buf[it, half, slot, part:, :].astype(jnp.int32).astype(F32)[:1, :]
            found.append(y * y * jnp.exp2(level * 0.125))
        return jnp.concatenate(found, axis=0)

    def numbers_of(buf, it, slot):
        row = buf[it, 0, slot, part:, :].astype(jnp.int32)[GROUP // 2 :, :]
        return row[:8, :]

    def weights(classes):
        out = jnp.zeros(classes.shape, F32)
        low, high = classes % size, classes // size
        for k in range(table_ref.shape[0]):
            table = jnp.broadcast_to(table_ref[k : k + 1, :], classes.shape)
            out = jnp.where(high == k, jnp.take_along_axis(table, low, axis=1), out)
        return out

    inputs[2].wait()
    for it in range(ITERS):
        picked[...] = jnp.dot(pick, price[...].astype(BF16), preferred_element_type=F32)
        for half in range(HALVES):
            route_terms(it == 0, half)
            encode(route_buf, it, half, me_l, flow_all)
            if it == 0 and half == 0:
                pl.semaphore_wait(barrier, n_link // 2 + n_flow - 1)
            for k, peer in enumerate(line + [partner]):
                copy = copy_of(route_buf.at[it, half], me_l, route_send.at[it, half], route_recv.at[it, half], k, peer, "link")
                copy.start()
                pending.append(copy)
        if it == 0:
            for copy in inputs[3:]:
                copy.wait()

            def own(s, carry):
                f = flow_smem[0, s]
                own_class[pl.ds(s, 1), :] = class_ref[pl.ds(f, 1), :]
                own_access[pl.ds(s, 1), :] = access_ref[pl.ds(f, 1), :]
                return carry

            lax.fori_loop(0, slots, own, 0, unroll=8)
            own_weight = weights(own_class[...])
            flow_col = column(flow_ref[...])

        route = jnp.zeros((slots, size), F32)

        def add(source, route):
            if it == 0:
                row = numbers_of(route_buf, it, source)
                flow_all[source] = row
                same = (flow_col == row[0:1, :].astype(F32)).astype(BF16)
                match[source, :, :slots] = same
                match[source, :, slots:] = same
            high, low = halves(decode(route_buf, it, source))
            both = jnp.concatenate([high, low], axis=0)
            if it == ITERS - 1:
                parts[source] = both
            return route + jnp.dot(match[source], both, preferred_element_type=F32)

        def await_route(half, source):
            copy_of(
                route_buf.at[it, half], source, route_send.at[it, half], route_recv.at[it, half], 0, partner, "link"
            ).wait_recv()

        route = add(me_l, route)
        for half in range(HALVES):
            for k, source in enumerate(line):
                await_route(half, source)
                copy = copy_of(
                    route_buf.at[it, half], source, route_send.at[it, half], route_recv.at[it, half],
                    n_link // 2 + k, partner, "link",
                )
                copy.start()
                pending.append(copy)
        for source in line:
            route = add(source, route)
        for source in [partner] + partner_line:
            for half in range(HALVES):
                await_route(half, source)
            route = add(source, route)
        rate_b[...] = (own_weight / (own_access[...] + route)).astype(BF16)
        for half in range(HALVES):
            load_terms(half)
            encode(load_buf, it, half, me_f, link_all)
            for k, peer in enumerate(flow_peers):
                copy = copy_of(load_buf.at[it, half], me_f, load_send.at[it, half], load_recv.at[it, half], k, peer, "flow")
                copy.start()
                pending.append(copy)
        if it == ITERS - 1:
            def rows(r, carry):
                at = pl.multiple_of(r * size, size)
                number = iota((size, slots), 0) + at
                route = jnp.zeros((size, size), F32)
                for d in range(n_link):
                    same = (number == flow_all[d, 0:1, :]).astype(F32).astype(BF16)
                    route = route + jnp.dot(
                        jnp.concatenate([same, same], axis=1), parts[d], preferred_element_type=F32
                    )
                block = pl.ds(at, size)
                rate_out[block, :] = weights(class_ref[block, :]) / (access_ref[block, :] + route)
                return carry

            lax.fori_loop(0, flow_blocks // size, rows, 0)

        load = jnp.zeros((link_blocks, size), F32)
        for k, source in enumerate([me_f] + flow_sources):
            if k:
                for half in range(HALVES):
                    copy_of(
                        load_buf.at[it, half], source, load_send.at[it, half], load_recv.at[it, half], 0, source, "flow"
                    ).wait_recv()
            if it == 0:
                row = numbers_of(load_buf, it, source)
                same = (iota((link_blocks, slots), 0) == row[0:1, :]).astype(F32).astype(BF16)
                spread[source, :, :slots] = same
                spread[source, :, slots:] = same
            high, low = halves(decode(load_buf, it, source))
            load = load + jnp.dot(
                spread[source], jnp.concatenate([high, low], axis=0), preferred_element_type=F32
            )
        new = price[...] * jnp.exp(STEP * (load / cap_ref[...] - 1.0))
        if it == ITERS - 1:
            price_out[...] = new
        else:
            price[...] = new
    for copy in pending:
        copy.wait_send()


def move(rate, price, rate_out, price_out, rate_held, price_held, sem):
    copies = []
    for source, held, target in ((rate, rate_held, rate_out), (price, price_held, price_out)):
        rows = source.shape[0] // 2
        for c in range(2):
            block, k = pl.ds(c * rows, rows), len(copies)
            copies.append((
                pltpu.make_async_copy(source.at[block], held.at[block], sem.at[0, k]),
                pltpu.make_async_copy(held.at[block], target.at[block], sem.at[1, k]),
            ))
    for first, _ in copies:
        first.start()
    for first, second in copies:
        first.wait()
        second.start()
    for _, second in copies:
        second.wait()


def on_device(n_flow, n_link, route_tiles, tile_count, tile_flow, tile_link, flow_class, class_weight, access_price,
              capacity, init_price):
    slots, _, size = route_tiles.shape
    flow_blocks, link_blocks = access_price.shape[0] // size, capacity.shape[0] // size
    vmem = pl.BlockSpec(memory_space=pltpu.VMEM)
    hbm = pl.BlockSpec(memory_space=pltpu.HBM)
    smem = pl.BlockSpec(memory_space=pltpu.SMEM)
    dma = pltpu.SemaphoreType.DMA
    rate, price = pl.pallas_call(
        functools.partial(kernel, n_flow, n_link),
        out_shape=(
            jax.ShapeDtypeStruct((flow_blocks, size), F32),
            jax.ShapeDtypeStruct((link_blocks, size), F32),
        ),
        in_specs=[hbm, smem, smem] + [hbm] * 7,
        out_specs=(vmem, vmem),
        scratch_shapes=[
            pltpu.VMEM((slots, size, size), BF16),
            pltpu.VMEM((n_link, 8, slots), jnp.int32),
            pltpu.VMEM((n_flow, 8, slots), jnp.int32),
            pltpu.VMEM((ITERS, HALVES, n_link, slots // HALVES + GROUP, size), jnp.int16),
            pltpu.VMEM((ITERS, HALVES, n_flow, slots // HALVES + GROUP, size), jnp.int16),
            pltpu.VMEM((slots, size), F32),
            pltpu.VMEM((slots, size), F32),
            pltpu.VMEM((slots, size), BF16),
            pltpu.VMEM((n_link, slots, 2 * slots), BF16),
            pltpu.VMEM((n_flow, link_blocks, 2 * slots), BF16),
            pltpu.VMEM((n_link, 2 * slots, size), BF16),
            pltpu.VMEM((slots, size), jnp.int32),
            pltpu.VMEM((slots, size), F32),
            pltpu.VMEM((link_blocks, size), F32),
            pltpu.VMEM((1, slots), jnp.int32),
            pltpu.VMEM((1, slots), jnp.int32),
            pltpu.VMEM((flow_blocks, size), jnp.int32),
            pltpu.VMEM((class_weight.shape[0] // size, size), F32),
            pltpu.VMEM((flow_blocks, size), F32),
            pltpu.VMEM((link_blocks, size), F32),
            dma((4,)),
            dma((7,)),
            dma((ITERS, HALVES, n_link)),
            dma((ITERS, HALVES, n_link)),
            dma((ITERS, HALVES, n_flow)),
            dma((ITERS, HALVES, n_flow)),
        ],
        compiler_params=pltpu.CompilerParams(
            collective_id=0, has_side_effects=True, vmem_limit_bytes=60 * 1024 * 1024
        ),
    )(
        route_tiles, tile_count, tile_flow, tile_flow, tile_link,
        flow_class.reshape(flow_blocks, size), class_weight.reshape(-1, size),
        access_price.reshape(flow_blocks, size), capacity.reshape(link_blocks, size),
        init_price.reshape(link_blocks, size),
    )
    rate, price = pl.pallas_call(
        move,
        out_shape=(
            jax.ShapeDtypeStruct((flow_blocks, size), F32),
            jax.ShapeDtypeStruct((link_blocks, size), F32),
        ),
        in_specs=[hbm, hbm],
        out_specs=(hbm, hbm),
        scratch_shapes=[
            pltpu.VMEM((flow_blocks, size), F32), pltpu.VMEM((link_blocks, size), F32), dma((2, 4)),
        ],
        compiler_params=pltpu.CompilerParams(vmem_limit_bytes=60 * 1024 * 1024),
    )(rate, price)
    return rate.reshape(-1), price.reshape(-1)


def solution(mesh):
    return jax.shard_map(
        functools.partial(on_device, mesh.shape["flow"], mesh.shape["link"]),
        mesh=mesh,
        in_specs=(
            P("flow", "link", None),
            P("flow", "link"),
            P("flow", "link"),
            P("flow", "link"),
            P("flow"),
            P(),
            P("flow"),
            P("link"),
            P("link"),
        ),
        out_specs=(P("flow"), P("link")),
        check_vma=False,
    )
```
